32 devices in a mesh: sector: 8 (over z, x), band: 4 (over y, core).
Axes of the slice: x: 2, y: 2, z: 4, core: 2. Of those that a mesh axis runs over, the one named last changes fastest.
Arguments:
- orbitals: bfloat16 [8, 32, 16, 4096], P('sector', None, None, 'band'), may hold values from -216 to 216
- potential: float32 [8, 32, 16], P('sector'), may hold values from 0.1 to 3
- near_points: int32 [128, 48], P('sector'), may hold values from 0 to 511
- near_values: bfloat16 [128, 48], P('sector'), may hold values from -0.875 to 0.875
- far_points: int32 [128, 16], P('sector'), may hold values from 0 to 511
- far_values: bfloat16 [128, 16], P('sector'), may hold values from -1.5 to 1.5
- atom_energy: float32 [128], P('sector'), may hold values from -1 to 2
Outputs:
- ham_panel: float32 [2048, 4096], P('sector', 'band')
- gram_panel: float32 [2048, 4096], P('sector', 'band')
The draws below stay inside these ranges and needn't reach their ends.
Inputs may be any that keep to these rules, and one draw needn't show every extreme that they name: `near_points`: indices of points of the owning slab. `far_points`: row block s names points of slab s's first plane, for the atoms owned by slab s - 1 (mod 8).
All inputs are finite; a program needn't handle non-finite values.
Results may differ from the reference program's by a relative error of at most 0.00039.
Values may be sent and summed in bfloat16 or wider, within the bound.
A program may use at most 64 MiB of HBM per device.

```python
import math
import jax
import jax.numpy as jnp
from jax import lax

A_DEV = 1
NR = 32
NZ = 16
TWIST = 3
ORB = 4096
PANEL = 2048
ATOM_DEV = 16
SUP_NEAR = 48
SUP_FAR = 16
NA = 8
PLANE = 512
PTS_DEV = 512
NG = 4096
ORB_DEV = 1024
PANEL_DEV = 512
ATOMS = 128
N_SECTOR = 8
N_BAND = 4


def draw_orbitals(key, part):
    key_noise = jax.random.fold_in(key, 11)
    key_fields = jax.random.fold_in(key, 12)
    key_mix = jax.random.fold_in(key, 13)
    key_rows = jax.random.fold_in(key, 14)
    key_cols = jax.random.fold_in(key, 15)
    noise = jnp.clip(jax.random.normal(key_noise, (NA, NR, NZ, ORB), jnp.float32), -4.0, 4.0)
    row_scale = jnp.exp(jax.random.uniform(key_rows, (NA, NR, NZ, 1), jnp.float32, jnp.log(0.3), jnp.log(3.0)))
    fields = jnp.clip(jax.random.normal(key_fields, (4, NA, NR, NZ, 1), jnp.float32), -4.0, 4.0)
    mixing = jnp.clip(0.5 * jax.random.normal(key_mix, (4, ORB), jnp.float32), -2.0, 2.0)
    col_scale = jnp.exp(jax.random.uniform(key_cols, (ORB,), jnp.float32, jnp.log(0.5), jnp.log(2.0)))
    total = noise
    total = total + fields[0] * mixing[0]
    total = total + fields[1] * mixing[1]
    total = total + fields[2] * mixing[2]
    total = total + fields[3] * mixing[3]
    return (row_scale * total * col_scale).astype(jnp.bfloat16)


def set_ends(drawn, own_key, low, high):
    index_at = [jax.random.randint(jax.random.fold_in(own_key, axis), (), 0, length) for axis, length in enumerate(drawn.shape)]
    widest = drawn.shape.index(max(drawn.shape))
    beside = index_at[:widest] + [(index_at[widest] + 1) % drawn.shape[widest]] + index_at[widest + 1:]
    return drawn.at[tuple(index_at)].set(low).at[tuple(beside)].set(high)


def block_scale(stream_key, extent, split, least, largest):
    loudness, own = 1.0, jax.random.fold_in(stream_key, 6)
    for dim, parts in split:
        heights = jnp.exp(jax.random.uniform(jax.random.fold_in(own, dim), (parts,), jnp.float32, least / len(split), largest / len(split)))
        loudness = loudness * jnp.repeat(heights, extent[dim] // parts).reshape([-1 if axis == dim else 1 for axis in range(len(extent))])
    return loudness


def gaussian(rng, dims, scale, reach, cuts=(), kind=jnp.bfloat16):
    result = scale * jax.random.normal(rng, dims, jnp.float32)
    if cuts:
        result = result * block_scale(rng, dims, cuts, -0.22, 0.18)
    return jnp.clip(result, -reach, reach).astype(kind)


def setup_inputs(seed: int = 0) -> dict:
    arg_keys = jax.random.split(jax.random.key(seed), 8)
    return {
        "orbitals": draw_orbitals(jax.random.fold_in(arg_keys[7], 71), 0),
        "potential": jnp.clip(jnp.exp(math.log(3.0) - 3.4011974 * jax.random.uniform(arg_keys[1], (NA, NR, NZ), jnp.float32) ** block_scale(arg_keys[1], (NA, NR, NZ), ((0, 8),), -0.2, 0.2)), 0.1, 3.0),
        "near_points": set_ends(jax.random.randint(arg_keys[2], (ATOMS, SUP_NEAR), 0, PTS_DEV), jax.random.fold_in(arg_keys[2], 1), 0, PTS_DEV - 1).astype(jnp.int32),
        "near_values": gaussian(arg_keys[3], (ATOMS, SUP_NEAR), SUP_NEAR ** -0.5, 0.875, ((0, 8),)),
        "far_points": set_ends(jax.random.randint(arg_keys[4], (ATOMS, SUP_FAR), 0, PLANE), jax.random.fold_in(arg_keys[4], 1), 0, PLANE - 1).astype(jnp.int32),
        "far_values": gaussian(arg_keys[5], (ATOMS, SUP_FAR), SUP_FAR ** -0.5, 1.5, ((0, 8),)),
        "atom_energy": jnp.clip(-1.0 + 3.0 * jax.random.uniform(arg_keys[6], (ATOMS,), jnp.float32) ** block_scale(arg_keys[6], (ATOMS,), ((0, 8),), -0.2, 0.2), -1.0, 2.0),
    }


CENTER = 6.0
HALF_SPAN = 3.0


def build_dense(points, values, width):
    column_ids = jnp.arange(width, dtype=jnp.int32)
    matches = (points[:, :, None] == column_ids[None, None, :]).astype(jnp.float32)
    return jnp.sum(matches * values.astype(jnp.float32)[:, :, None], axis=1).astype(jnp.bfloat16)


def apply_operator(field_in, potential, near_dense, far_dense, atom_energy):
    wavefunc = field_in.astype(jnp.float32)
    upper_plane = jnp.roll(wavefunc[0], -TWIST, axis=1)
    lower_plane = jnp.roll(wavefunc[-1], TWIST, axis=1)
    angular = jnp.concatenate([wavefunc[1:], upper_plane[None]], 0) + jnp.concatenate([lower_plane[None], wavefunc[:-1]], 0) - 2.0 * wavefunc
    zero_rim = jnp.zeros_like(wavefunc[:, :1])
    outer_rad = jnp.concatenate([wavefunc[:, 1:], zero_rim], 1)
    inner_rad = jnp.concatenate([zero_rim, wavefunc[:, :-1]], 1)
    radius = (NR + jnp.arange(NR, dtype=jnp.float32))[None, :, None, None]
    radial = outer_rad + inner_rad - 2.0 * wavefunc + (outer_rad - inner_rad) / (2.0 * radius)
    axial_sum = jnp.roll(wavefunc, 1, axis=2) + jnp.roll(wavefunc, -1, axis=2) - 2.0 * wavefunc
    weight = (NR / radius) ** 2
    kinetic = -0.5 * (radial + axial_sum + weight * angular)
    slabs = field_in.reshape(N_SECTOR, PTS_DEV, -1).astype(jnp.float32)
    near_f = near_dense.astype(jnp.float32)
    far_f = far_dense.astype(jnp.float32)
    near_coef = jnp.einsum('sap,spo->sao', near_f, slabs)
    first_planes = field_in.reshape(N_SECTOR, A_DEV, PLANE, -1)[:, 0].astype(jnp.float32)
    far_coef = jnp.einsum('sap,spo->sao', far_f, first_planes)
    coeffs = near_coef + jnp.roll(far_coef, -1, axis=0)
    scaled = atom_energy.reshape(N_SECTOR, ATOM_DEV)[:, :, None] * coeffs
    spread = jnp.einsum('sap,sao->spo', near_f, scaled, precision=lax.Precision.HIGHEST)
    back_add = jnp.einsum('sap,sao->spo', far_f, jnp.roll(scaled, 1, axis=0), precision=lax.Precision.HIGHEST)
    spread = spread.reshape(N_SECTOR, A_DEV, PLANE, -1)
    spread = spread.at[:, 0].add(back_add)
    nonlocal_term = spread.reshape(NA, NR, NZ, -1)
    return kinetic + potential[..., None] * wavefunc + nonlocal_term


def reference(orbitals, potential, near_points, near_values, far_points, far_values, atom_energy):
    near_dense = lax.map(lambda pair: build_dense(pair[0], pair[1], PTS_DEV),
                         (near_points.reshape(N_SECTOR, ATOM_DEV, SUP_NEAR), near_values.reshape(N_SECTOR, ATOM_DEV, SUP_NEAR)))
    far_dense = lax.map(lambda pair: build_dense(pair[0], pair[1], PLANE),
                        (far_points.reshape(N_SECTOR, ATOM_DEV, SUP_FAR), far_values.reshape(N_SECTOR, ATOM_DEV, SUP_FAR)))
    blocks = orbitals.reshape(NA, NR, NZ, N_BAND, ORB_DEV).transpose(3, 0, 1, 2, 4)

    def operate(field_in):
        return apply_operator(field_in, potential, near_dense, far_dense, atom_energy)

    def filter_block(block):
        block32 = block.astype(jnp.float32)
        first = ((operate(block) - CENTER * block32) / HALF_SPAN).astype(jnp.bfloat16)
        filtered = (2.0 * (operate(first) - CENTER * first.astype(jnp.float32)) / HALF_SPAN - block32).astype(jnp.bfloat16)
        image = operate(filtered).astype(jnp.bfloat16)
        return filtered.reshape(NG, ORB_DEV), image.reshape(NG, ORB_DEV)

    filtered_all, images_all = lax.map(filter_block, blocks)
    panel = filtered_all[:, :, :PANEL_DEV].transpose(1, 0, 2).reshape(NG, PANEL).astype(jnp.float32)

    def project(pair):
        filtered_b, image_b = pair
        ham_b = jnp.dot(panel.T, image_b.astype(jnp.float32), precision=lax.Precision.HIGHEST)
        gram_b = jnp.dot(panel.T, filtered_b.astype(jnp.float32), precision=lax.Precision.HIGHEST)
        return ham_b, gram_b

    hams, grams = lax.map(project, (filtered_all, images_all))
    ham_panel = hams.transpose(1, 0, 2).reshape(PANEL, ORB) / NG
    gram_panel = grams.transpose(1, 0, 2).reshape(PANEL, ORB) / NG
    return ham_panel, gram_panel
```

```python
import functools

import jax
import jax.numpy as jnp
from jax import lax
from jax.experimental import pallas as pl
from jax.experimental.pallas import tpu as pltpu
from jax.sharding import PartitionSpec as P

MESH = pl.DeviceIdType.MESH
F32 = jnp.float32
BF16 = jnp.bfloat16

TWIST = 3
PANEL = 2048
CENTER = 6.0
HALF_SPAN = 3.0
LANES = 128
SKEW = 2


def build_dense(points, values, width):
    column_ids = jnp.arange(width, dtype=jnp.int32)
    matches = (points[:, :, None] == column_ids[None, None, :]).astype(F32)
    return jnp.sum(matches * values.astype(F32)[:, :, None], axis=1).astype(BF16)


def widen(tile, width):
    return jnp.concatenate([tile] * (width // LANES), axis=1) if width > LANES else tile


def kernel(n, nb, nr, nz, atoms, chunk, orb, bund, shifts, ham, gram,
           O, A, F, I, BB, W, G, D, CO, SP, ACC, PB, PT, PH, PG,
           send_sem, recv_sem, bsend_sem, brecv_sem, psend_sem, precv_sem):
    plane, cols = orb.shape
    rows = ham.shape[0]
    half = plane // 2
    chunks = cols // chunk
    steps = n // 2
    panel_dev = PANEL // nb
    pw = PB.shape[2]
    pieces = pw // LANES
    groups = panel_dev // pw
    order = [m * pieces + j for j in range(pieces) for m in range(groups)]
    order += list(range(panel_dev // LANES, cols // LANES))
    s = lax.axis_index("sector")
    b = lax.axis_index("band")

    def ring_sector(r):
        r = lax.rem(r + 2 * n, n)
        return jnp.where(r < n // 2, 2 * r, 2 * (n - 1 - r) + 1)

    pos = jnp.where(lax.rem(s, 2) == 0, s // 2, n - 1 - s // 2)
    ahead = ring_sector(pos + 1)
    behind = ring_sector(pos - 1)
    panel_row = s * rows
    owner = panel_row // panel_dev
    offset = panel_row - owner * panel_dev
    group = offset // pw
    sub = pl.multiple_of(offset - group * pw, 8)

    barrier = pltpu.get_barrier_semaphore()
    pl.semaphore_signal(barrier, inc=1, device_id={"sector": ahead}, device_id_type=MESH)
    pl.semaphore_signal(barrier, inc=1, device_id={"sector": behind}, device_id_type=MESH)
    for d in range(1, nb):
        pl.semaphore_signal(barrier, inc=1, device_id={"band": lax.rem(b + d, nb)}, device_id_type=MESH)

    for j, source in enumerate(order):
        O[s + 1, nz:nz + plane, j * LANES:(j + 1) * LANES] = orb[:, source * LANES:(source + 1) * LANES]
    BB[s] = bund[...]
    pl.semaphore_wait(barrier, 2 + nb - 1)

    def block_copy(c, k, way):
        blk = ring_sector(pos - k if way == 0 else pos + k)
        if k == steps - 1:
            span = pl.ds(nz + way * half, half)
        else:
            span = pl.ds(nz, plane)
        ref = O.at[blk + 1, span, pl.ds(c * chunk, chunk)]
        return pltpu.make_async_remote_copy(
            src_ref=ref, dst_ref=ref, send_sem=send_sem.at[way, c, k], recv_sem=recv_sem.at[way, c, k],
            device_id={"sector": ahead if way == 0 else behind}, device_id_type=MESH)

    def bundle_copy(k, way):
        blk = ring_sector(pos - k if way == 0 else pos + k)
        ref = BB.at[blk]
        return pltpu.make_async_remote_copy(
            src_ref=ref, dst_ref=ref, send_sem=bsend_sem.at[way, k], recv_sem=brecv_sem.at[way, k],
            device_id={"sector": ahead if way == 0 else behind}, device_id_type=MESH)

    def block_wait(c, k, way):
        blk = ring_sector(pos - k - 1 if way == 0 else pos + k + 1)
        if k == steps - 1:
            span = pl.ds(nz + way * half, half)
        else:
            span = pl.ds(nz, plane)
        ref = O.at[blk + 1, span, pl.ds(c * chunk, chunk)]
        pltpu.make_async_remote_copy(
            src_ref=ref, dst_ref=ref, send_sem=send_sem.at[way, c, k], recv_sem=recv_sem.at[way, c, k],
            device_id={"sector": ahead if way == 0 else behind}, device_id_type=MESH).wait_recv()

    def bundle_wait(k, way):
        blk = ring_sector(pos - k - 1 if way == 0 else pos + k + 1)
        ref = BB.at[blk]
        pltpu.make_async_remote_copy(
            src_ref=ref, dst_ref=ref, send_sem=bsend_sem.at[way, k], recv_sem=brecv_sem.at[way, k],
            device_id={"sector": ahead if way == 0 else behind}, device_id_type=MESH).wait_recv()

    def bundle_ways(k):
        return (0,) if k == steps - 1 else (0, 1)

    def panel_copy(j, d):
        lane = pl.multiple_of((j * groups + group) * LANES, LANES)
        return pltpu.make_async_remote_copy(
            src_ref=F.at[pl.ds(1, n), pl.ds(nz, plane), pl.ds(lane, LANES)],
            dst_ref=PB.at[:, :, pl.ds(j * LANES, LANES)],
            send_sem=psend_sem.at[j, d], recv_sem=precv_sem.at[j],
            device_id={"band": lax.rem(b + d, nb)}, device_id_type=MESH)

    for way in bundle_ways(0):
        bundle_copy(0, way).start()
    for c in range(min(2, chunks)):
        for way in (0, 1):
            block_copy(c, 0, way).start()

    for ref in (O, F):
        @pl.loop(0, n)
        def _(p):
            ref[p + 1, 0:nz, :] = jnp.zeros((nz, cols), BF16)
            ref[p + 1, nz + plane:nz + plane + nz, :] = jnp.zeros((nz, cols), BF16)

    @pl.loop(0, n)
    def _(p):
        A[p + 1, 0:nz, :] = jnp.zeros((nz, chunk), BF16)
        A[p + 1, nz + plane:nz + plane + nz, :] = jnp.zeros((nz, chunk), BF16)
        SP[p] = jnp.zeros(SP.shape[1:], BF16)

    def setup():
        @pl.loop(0, n)
        def _(p):
            dense = BB[p, 0:2 * atoms, :]
            W[p] = dense.astype(BF16)
            copies = LANES // (2 * atoms)
            G[p] = jnp.concatenate([dense] * copies, axis=0).T.astype(BF16)
            local = jnp.broadcast_to(BB[p, 3 * atoms:3 * atoms + 1, :], (LANES, plane)).T
            for i in range(nr):
                w = (nr / (nr + i)) ** 2
                D[p, i * nz:(i + 1) * nz, :] = local[i * nz:(i + 1) * nz] + (2.0 + w)

    def prepare(v, cs):
        for h in range(2):
            r = nz + h * half
            v[0, r:r + half, cs] = jnp.dot(shifts[1], v[n, r:r + half, cs], preferred_element_type=F32).astype(BF16)
            v[n + 1, r:r + half, cs] = jnp.dot(shifts[2], v[1, r:r + half, cs], preferred_element_type=F32).astype(BF16)

        @pl.loop(0, n)
        def _(p):
            CO[p] = jnp.dot(W[p], v[p + 1, nz:nz + plane, cs], preferred_element_type=F32)

        @pl.loop(0, n)
        def _(p):
            after = lax.rem(p + 1, n)
            energy = widen(BB[p, 2 * atoms:3 * atoms, 0:LANES], chunk)
            rest = energy * (CO[p, 0:atoms, :] + CO[after, atoms:2 * atoms, :])
            for term in range(3):
                part = rest.astype(BF16)
                rest = rest - part.astype(F32)
                r = term * 2 * atoms
                SP[p, r:r + atoms, :] = part
                SP[after, r + atoms:r + 2 * atoms, :] = part

    def operate(v, cs, finish):
        prepare(v, cs)

        @pl.loop(0, n)
        def _(p):
            for h in range(2):
                base = nz + h * half
                ACC[...] = (
                    jnp.dot(shifts[0], v[p + 1, base:base + half, cs], preferred_element_type=F32)
                    + jnp.dot(G[p, h * half:(h + 1) * half, :], SP[p], preferred_element_type=F32))
                for i in range(half // nz):
                    ri = nr + h * (half // nz) + i
                    r = base + i * nz
                    centre = v[p + 1, r:r + nz, cs].astype(F32)
                    outer = v[p + 1, r + nz:r + 2 * nz, cs].astype(F32)
                    inner = v[p + 1, r - nz:r, cs].astype(F32)
                    sides = v[p + 2, r:r + nz, cs].astype(F32) + v[p, r:r + nz, cs].astype(F32)
                    local = widen(D[p, r - nz:r, :], chunk)
                    value = (
                        ACC[i * nz:(i + 1) * nz, :]
                        + (-0.5 * (1.0 + 1.0 / (2.0 * ri))) * outer
                        + (-0.5 * (1.0 - 1.0 / (2.0 * ri))) * inner
                        + (-0.5 * (nr / ri) ** 2) * sides
                        + local * centre)
                    finish(p, r, centre, value)

    def stage_first(c):
        cs = slice(c * chunk, (c + 1) * chunk)

        def finish(p, r, centre, value):
            A[p + 1, r:r + nz, :] = ((value - CENTER * centre) * (1.0 / HALF_SPAN)).astype(BF16)

        operate_from(O, cs, finish)

    def operate_from(v, cs, finish):
        operate(v, cs, finish)

    def stage_filtered(c):
        cs = slice(c * chunk, (c + 1) * chunk)

        def finish(p, r, centre, value):
            start = O[p + 1, r:r + nz, cs].astype(F32)
            F[p + 1, r:r + nz, cs] = (
                (value - CENTER * centre) * (2.0 / HALF_SPAN) - start).astype(BF16)

        operate(A, slice(0, chunk), finish)

    def panel_send(j):
        @pl.when(b == owner)
        def _():
            for d in range(1, nb):
                panel_copy(j, d).start()
            lane = pl.multiple_of((j * groups + group) * LANES, LANES)

            @pl.loop(0, n)
            def _(p):
                PB[p, :, j * LANES:(j + 1) * LANES] = F[p + 1, nz:nz + plane, pl.ds(lane, LANES)]

    def stage_image(c):
        cs = slice(c * chunk, (c + 1) * chunk)

        def finish(p, r, centre, value):
            I[p, r - nz:r, cs] = value.astype(BF16)

        operate(F, cs, finish)

    def panel_ready():
        @pl.when(b != owner)
        def _():
            for j in range(pieces):
                panel_copy(j, 1).wait_recv()

        @pl.loop(0, n)
        def _(p):
            PT[p] = PB[p].T

    def project(c):
        cs = slice(c * chunk, (c + 1) * chunk)
        PG[...] = jnp.zeros(PG.shape, F32)
        PH[...] = jnp.zeros(PH.shape, F32)

        @pl.loop(0, n)
        def _(p):
            PG[...] += jnp.dot(PT[p], F[p + 1, nz:nz + plane, cs], preferred_element_type=F32)
            PH[...] += jnp.dot(PT[p], I[p, :, cs], preferred_element_type=F32)

        scale = 1.0 / (plane * n)
        for q in range(chunk // LANES):
            source = order[c * (chunk // LANES) + q]
            place = slice(source * LANES, (source + 1) * LANES)
            lanes = slice(q * LANES, (q + 1) * LANES)
            gram[:, place] = PG[pl.ds(sub, rows), lanes] * scale
            ham[:, place] = PH[pl.ds(sub, rows), lanes] * scale

    piece_chunk = [((j + 1) * groups * LANES - 1) // chunk for j in range(pieces)]
    work = {}
    last_slot = SKEW * (chunks - 1) + steps - 1
    for c in range(chunks):
        t = SKEW * c + steps - 1
        early, late = work.setdefault(t, []), work.setdefault(t + 1, [])
        if c == 0:
            early.append(setup)
        early.append(functools.partial(stage_first, c))
        early.append(functools.partial(stage_filtered, c))
        for j in range(pieces):
            if piece_chunk[j] == c:
                early.append(functools.partial(panel_send, j))
        late.append(functools.partial(stage_image, c))
    tail = []
    for t in range(last_slot + 1):
        if t < steps:
            for way in bundle_ways(t):
                bundle_wait(t, way)
            if t + 1 < steps:
                for way in bundle_ways(t + 1):
                    bundle_copy(t + 1, way).start()
        for c in range(chunks):
            k = t - SKEW * c
            if 0 <= k < steps:
                for way in (0, 1):
                    block_wait(c, k, way)
                    if k + 1 < steps:
                        block_copy(c, k + 1, way).start()
            if c >= 2 and t == SKEW * (c - 1) - 1:
                for way in (0, 1):
                    block_copy(c, 0, way).start()
        for item in work.get(t, []):
            item()
    for t in sorted(work):
        if t > last_slot:
            for item in work[t]:
                item()
    panel_ready()
    for c in range(chunks):
        project(c)

    for k in range(steps):
        for way in bundle_ways(k):
            bundle_copy(k, way).wait_send()
        for c in range(chunks):
            for way in (0, 1):
                block_copy(c, k, way).wait_send()

    @pl.when(b == owner)
    def _():
        for j in range(pieces):
            for d in range(1, nb):
                panel_copy(j, d).wait_send()


def shift_matrices(size, nz):
    row = jnp.arange(size)[:, None]
    col = jnp.arange(size)[None, :]
    same = row // nz == col // nz
    gap = (col - row) % nz
    near = jnp.where(same & ((gap == 1) | (gap == nz - 1)), -0.5, 0.0)
    lower = jnp.where(same & (gap == nz - TWIST), 1.0, 0.0)
    upper = jnp.where(same & (gap == TWIST), 1.0, 0.0)
    return jnp.stack([near, lower, upper]).astype(BF16)


def on_device(n, nb, orbitals, potential, near_points, near_values, far_points, far_values, atom_energy):
    _, nr, nz, cols = orbitals.shape
    plane = nr * nz
    atoms = near_points.shape[0]
    near = build_dense(near_points, near_values, plane).astype(F32)
    far = build_dense(far_points, far_values, plane).astype(F32)
    energy = jnp.broadcast_to(atom_energy[:, None], (atoms, plane))
    local = jnp.broadcast_to(potential.reshape(1, plane), (8, plane))
    bund = jnp.concatenate([near, far, energy, local], axis=0)
    shifts = shift_matrices(plane // 2, nz)
    chunk = 256 if cols >= 512 else LANES
    chunks = cols // chunk
    rows = PANEL // n
    pw = max(rows, LANES)
    pieces = pw // LANES
    steps = n // 2
    tall = plane + 2 * nz
    vmem = pl.BlockSpec(memory_space=pltpu.VMEM)
    return pl.pallas_call(
        functools.partial(kernel, n, nb, nr, nz, atoms, chunk),
        out_shape=(jax.ShapeDtypeStruct((rows, cols), F32),) * 2,
        in_specs=[vmem] * 3,
        out_specs=(vmem,) * 2,
        scratch_shapes=[
            pltpu.VMEM((n + 2, tall, cols), BF16),
            pltpu.VMEM((n + 2, tall, chunk), BF16),
            pltpu.VMEM((n + 2, tall, cols), BF16),
            pltpu.VMEM((n, plane, cols), BF16),
            pltpu.VMEM((n,) + bund.shape, F32),
            pltpu.VMEM((n, 2 * atoms, plane), BF16),
            pltpu.VMEM((n, plane, LANES), BF16),
            pltpu.VMEM((n, plane, LANES), F32),
            pltpu.VMEM((n, 2 * atoms, chunk), F32),
            pltpu.VMEM((n, LANES, chunk), BF16),
            pltpu.VMEM((plane // 2, chunk), F32),
            pltpu.VMEM((n, plane, pw), BF16),
            pltpu.VMEM((n, pw, plane), BF16),
            pltpu.VMEM((pw, chunk), F32),
            pltpu.VMEM((pw, chunk), F32),
            pltpu.SemaphoreType.DMA((2, chunks, steps)),
            pltpu.SemaphoreType.DMA((2, chunks, steps)),
            pltpu.SemaphoreType.DMA((2, steps)),
            pltpu.SemaphoreType.DMA((2, steps)),
            pltpu.SemaphoreType.DMA((pieces, nb)),
            pltpu.SemaphoreType.DMA((pieces,)),
        ],
        compiler_params=pltpu.CompilerParams(
            collective_id=0, has_side_effects=True, vmem_limit_bytes=60 * 2 ** 20
        ),
    )(orbitals.reshape(plane, cols), bund, shifts)


def solution(mesh):
    n, nb = mesh.shape["sector"], mesh.shape["band"]
    return jax.shard_map(
        functools.partial(on_device, n, nb),
        mesh=mesh,
        in_specs=(
            P("sector", None, None, "band"),
            P("sector", None, None),
            P("sector", None),
            P("sector", None),
            P("sector", None),
            P("sector", None),
            P("sector"),
        ),
        out_specs=(P("sector", "band"), P("sector", "band")),
        check_vma=False,
    )
```

```python
import functools

import jax
import jax.numpy as jnp
from jax import lax
from jax.experimental import pallas as pl
from jax.experimental.pallas import tpu as pltpu
from jax.sharding import PartitionSpec as P

MESH = pl.DeviceIdType.MESH
F32 = jnp.float32
BF16 = jnp.bfloat16

TWIST = 3
PANEL = 2048
CENTER = 6.0
HALF_SPAN = 3.0
LANES = 128
SKEW = 2


def build_dense(points, values, width):
    column_ids = jnp.arange(width, dtype=jnp.int32)
    matches = (points[:, :, None] == column_ids[None, None, :]).astype(F32)
    return jnp.sum(matches * values.astype(F32)[:, :, None], axis=1).astype(BF16)


def widen(tile, width):
    return jnp.concatenate([tile] * (width // LANES), axis=1) if width > LANES else tile


def kernel(n, nb, nr, nz, atoms, chunk, batch, orb, bund, shifts, ham, gram,
           O, A, F, I, BB, W, G, D, CO, SP, ACC, PB, PT, PH, PG, RH, RG,
           xs, xr, zs, zr, bxs, bxr, bzs, bzr, ps, pr, os, orr):
    plane, cols = orb.shape
    rows = ham.shape[0]
    half = plane // 2
    mine = cols // 2
    chunks = mine // chunk
    batches = mine // batch
    levels = n // 2
    panel_dev = PANEL // nb
    panel_blocks = panel_dev // LANES
    pieces = max(panel_blocks // 2, 1)
    both = panel_blocks >= 2
    order = list(range(pieces)) + ([panel_blocks + j for j in range(pieces)] if both else [])
    s = lax.axis_index("sector")
    b = lax.axis_index("band")
    x = lax.rem(s, 2)
    level = s // 2
    partner = s + 1 - 2 * x
    above, below = s + 2, s - 2
    core = lax.rem(b, 2)
    sibling = b + 1 - 2 * core
    owner = level

    def source_lane(j, side):
        return pl.multiple_of((order[j] + side * pieces) * LANES, LANES)

    def remote(src, dst, send, recv, **device):
        return pltpu.make_async_remote_copy(
            src_ref=src, dst_ref=dst, send_sem=send, recv_sem=recv, device_id=device, device_id_type=MESH)

    barrier = pltpu.get_barrier_semaphore()
    pl.semaphore_signal(barrier, inc=1, device_id={"sector": partner}, device_id_type=MESH)

    @pl.when(level < levels - 1)
    def _():
        pl.semaphore_signal(barrier, inc=1, device_id={"sector": above}, device_id_type=MESH)

    @pl.when(level > 0)
    def _():
        pl.semaphore_signal(barrier, inc=1, device_id={"sector": below}, device_id_type=MESH)

    for d in range(1, nb):
        pl.semaphore_signal(barrier, inc=1, device_id={"band": lax.rem(b + d, nb)}, device_id_type=MESH)

    for j in range(mine // LANES):
        O[s + 1, nz:nz + plane, j * LANES:(j + 1) * LANES] = orb[:, pl.ds(source_lane(j, x), LANES)]
    BB[s] = bund[...]
    ends = jnp.where(level == 0, 1, 0) + jnp.where(level == levels - 1, 1, 0)
    pl.semaphore_wait(barrier, nb + 2 - ends)

    per = chunk // LANES

    def cross(c):
        return remote(orb.at[:, pl.ds(source_lane(c * per, 1 - x), chunk)],
                      O.at[s + 1, pl.ds(nz, plane), pl.ds(c * chunk, chunk)],
                      xs.at[c], xr.at[c], sector=partner)

    def cross_wait(c):
        remote(orb.at[:, pl.ds(source_lane(c * per, x), chunk)],
               O.at[partner + 1, pl.ds(nz, plane), pl.ds(c * chunk, chunk)],
               xs.at[c], xr.at[c], sector=partner).wait_recv()

    def bundle_cross():
        return remote(BB.at[s], BB.at[s], bxs, bxr, sector=partner)

    def bundle_cross_wait():
        remote(BB.at[partner], BB.at[partner], bxs, bxr, sector=partner).wait_recv()

    def hop_parts(way, lv):
        if way == 0:
            return above
        return below

    def block_hop(c, lv, k, way):
        ref = O.at[pl.ds(2 * lv + 1, 2), pl.ds(nz, plane), pl.ds(c * chunk, chunk)]
        return remote(ref, ref, zs.at[way, c, k], zr.at[way, c, k], sector=hop_parts(way, lv))

    def bundle_hop(lv, k, way):
        ref = BB.at[pl.ds(2 * lv, 2)]
        return remote(ref, ref, bzs.at[way, k], bzr.at[way, k], sector=hop_parts(way, lv))

    def sends(make, k, act):
        @pl.when((level - k >= 0) & (level < levels - 1))
        def _():
            act(make(level - k, k, 0))

        @pl.when((level + k < levels) & (level > 0))
        def _():
            act(make(level + k, k, 1))

    def receives(make, k):
        @pl.when(level - 1 - k >= 0)
        def _():
            make(level - 1 - k, k, 0).wait_recv()

        @pl.when(level + 1 + k < levels)
        def _():
            make(level + 1 + k, k, 1).wait_recv()

    def chunk_hop(c):
        return functools.partial(block_hop, c)

    bundle_cross().start()
    for c in range(chunks):
        cross(c).start()

    for ref in (O, F):
        @pl.loop(0, n)
        def _(p):
            ref[p + 1, 0:nz, :] = jnp.zeros((nz, mine), BF16)
            ref[p + 1, nz + plane:nz + plane + nz, :] = jnp.zeros((nz, mine), BF16)

    @pl.loop(0, n)
    def _(p):
        A[p + 1, 0:nz, :] = jnp.zeros((nz, chunk), BF16)
        A[p + 1, nz + plane:nz + plane + nz, :] = jnp.zeros((nz, chunk), BF16)
        SP[p] = jnp.zeros(SP.shape[1:], BF16)

    def setup():
        @pl.loop(0, n)
        def _(p):
            dense = BB[p, 0:2 * atoms, :]
            W[p] = dense.astype(BF16)
            copies = LANES // (2 * atoms)
            G[p] = jnp.concatenate([dense] * copies, axis=0).T.astype(BF16)
            local = jnp.broadcast_to(BB[p, 3 * atoms:3 * atoms + 1, :], (LANES, plane)).T
            for i in range(nr):
                w = (nr / (nr + i)) ** 2
                D[p, i * nz:(i + 1) * nz, :] = local[i * nz:(i + 1) * nz] + (2.0 + w)

    def prepare(v, cs):
        for h in range(2):
            r = nz + h * half
            v[0, r:r + half, cs] = jnp.dot(shifts[1], v[n, r:r + half, cs], preferred_element_type=F32).astype(BF16)
            v[n + 1, r:r + half, cs] = jnp.dot(shifts[2], v[1, r:r + half, cs], preferred_element_type=F32).astype(BF16)

        @pl.loop(0, n, unroll=4)
        def _(p):
            CO[p] = jnp.dot(W[p], v[p + 1, nz:nz + plane, cs], preferred_element_type=F32)

        @pl.loop(0, n)
        def _(p):
            after = lax.rem(p + 1, n)
            energy = widen(BB[p, 2 * atoms:3 * atoms, 0:LANES], chunk)
            rest = energy * (CO[p, 0:atoms, :] + CO[after, atoms:2 * atoms, :])
            for term in range(3):
                part = rest.astype(BF16)
                rest = rest - part.astype(F32)
                r = term * 2 * atoms
                SP[p, r:r + atoms, :] = part
                SP[after, r + atoms:r + 2 * atoms, :] = part

    def operate(v, cs, finish):
        prepare(v, cs)

        @pl.loop(0, n)
        def _(p):
            for h in range(2):
                base = nz + h * half
                ACC[h] = (
                    jnp.dot(shifts[0], v[p + 1, base:base + half, cs], preferred_element_type=F32)
                    + jnp.dot(G[p, h * half:(h + 1) * half, :], SP[p], preferred_element_type=F32))
            inner = None
            centre = v[p + 1, nz:2 * nz, cs].astype(F32)
            for i in range(nr):
                ri = nr + i
                r = nz + i * nz
                q = i * nz - (half if i * nz >= half else 0)
                outer = v[p + 1, r + nz:r + 2 * nz, cs].astype(F32) if i < nr - 1 else None
                sides = v[p + 2, r:r + nz, cs].astype(F32) + v[p, r:r + nz, cs].astype(F32)
                local = widen(D[p, r - nz:r, :], chunk)
                value = (
                    ACC[i * nz // half, q:q + nz, :]
                    + (-0.5 * (nr / ri) ** 2) * sides
                    + local * centre)
                if outer is not None:
                    value = value + (-0.5 * (1.0 + 1.0 / (2.0 * ri))) * outer
                if inner is not None:
                    value = value + (-0.5 * (1.0 - 1.0 / (2.0 * ri))) * inner
                finish(p, r, centre, value)
                inner, centre = centre, outer

    def stage_first(c):
        cs = slice(c * chunk, (c + 1) * chunk)

        def finish(p, r, centre, value):
            A[p + 1, r:r + nz, :] = ((value - CENTER * centre) * (1.0 / HALF_SPAN)).astype(BF16)

        operate(O, cs, finish)

    def stage_filtered(c):
        cs = slice(c * chunk, (c + 1) * chunk)

        def finish(p, r, centre, value):
            start = O[p + 1, r:r + nz, cs].astype(F32)
            F[p + 1, r:r + nz, cs] = (
                (value - CENTER * centre) * (2.0 / HALF_SPAN) - start).astype(BF16)

        operate(A, slice(0, chunk), finish)

    def stage_image(c):
        cs = slice(c * chunk, (c + 1) * chunk)

        def finish(p, r, centre, value):
            I[p, r - nz:r, cs] = value.astype(BF16)

        operate(F, cs, finish)

    part = n // 2

    def panel_at(j, side, which):
        lane = pl.multiple_of((j + side * pieces) * LANES, LANES)
        return PB.at[pl.ds(which * part, part), :, pl.ds(lane, LANES)]

    def panel_out(j, d):
        to = lax.rem(b + d, nb)
        which = lax.rem(to, 2)
        return remote(F.at[pl.ds(1 + which * part, part), pl.ds(nz, plane), pl.ds(j * LANES, LANES)],
                      panel_at(j, x, which), ps.at[0, j, d], pr.at[0, j], band=to)

    def panel_cross(j, side):
        return remote(panel_at(j, side, core), panel_at(j, side, core), ps.at[1, j, 0], pr.at[1, j], sector=partner)

    def panel_pair(j, side, which, own):
        k = 2 if own else 3
        return remote(panel_at(j, side, which), panel_at(j, side, which), ps.at[k, j, 0], pr.at[k, j], band=sibling)

    def when_own(f):
        if both:
            f()
        else:
            pl.when(x == 0)(f)

    def when_other(f):
        if both:
            f()
        else:
            pl.when(x == 1)(f)

    def panel_one(j):
        def go():
            @pl.when(b == owner)
            def _():
                for d in range(1, nb):
                    panel_out(j, d).start()
                lane = pl.multiple_of((j + x * pieces) * LANES, LANES)

                @pl.loop(0, part)
                def _(p):
                    PB[core * part + p, :, pl.ds(lane, LANES)] = (
                        F[1 + core * part + p, nz:nz + plane, j * LANES:(j + 1) * LANES])
        when_own(go)

    def panel_two(j):
        def go():
            @pl.when(b != owner)
            def _():
                remote(panel_at(j, x, core), panel_at(j, x, core), ps.at[0, j, 0], pr.at[0, j], band=sibling).wait_recv()
            panel_cross(j, x).start()
            panel_pair(j, x, core, True).start()
        when_own(go)

    def panel_three(j):
        def go():
            panel_cross(j, 1 - x).wait_recv()
            panel_pair(j, 1 - x, core, False).start()
        when_other(go)

    def panel_ready():
        for j in range(pieces):
            when_own(lambda: panel_pair(j, x, 1 - core, True).wait_recv())
            when_other(lambda: panel_pair(j, 1 - x, 1 - core, False).wait_recv())

        @pl.loop(0, n)
        def _(p):
            PT[p] = PB[p].T

    def panel_done():
        for j in range(pieces):
            def own():
                @pl.when(b == owner)
                def _():
                    for d in range(1, nb):
                        panel_out(j, d).wait_send()
                panel_cross(j, x).wait_send()
                panel_pair(j, x, core, True).wait_send()
            when_own(own)
            when_other(lambda: panel_pair(j, 1 - x, core, False).wait_send())

    scale = 1.0 / (plane * n)

    def result_copies(g):
        theirs = pl.ds(pl.multiple_of((1 - x) * rows, 8), rows)
        return (remote(PH.at[g, theirs], RH.at[g], os.at[0, g], orr.at[0, g], sector=partner),
                remote(PG.at[g, theirs], RG.at[g], os.at[1, g], orr.at[1, g], sector=partner))

    def project(g):
        cs = slice(g * batch, (g + 1) * batch)
        PG[g] = jnp.dot(PT[0], F[1, nz:nz + plane, cs], preferred_element_type=F32)
        PH[g] = jnp.dot(PT[0], I[0, :, cs], preferred_element_type=F32)

        @pl.loop(1, n)
        def _(p):
            PG[g] += jnp.dot(PT[p], F[p + 1, nz:nz + plane, cs], preferred_element_type=F32)
            PH[g] += jnp.dot(PT[p], I[p, :, cs], preferred_element_type=F32)

        for copy in result_copies(g):
            copy.start()
        ours = pl.ds(pl.multiple_of(x * rows, 8), rows)
        for q in range(batch // LANES):
            place = pl.ds(source_lane(g * (batch // LANES) + q, x), LANES)
            lanes = slice(q * LANES, (q + 1) * LANES)
            gram[:, place] = PG[g, ours, lanes] * scale
            ham[:, place] = PH[g, ours, lanes] * scale

    def collect(g):
        for copy in result_copies(g):
            copy.wait_recv()
        for q in range(batch // LANES):
            place = pl.ds(source_lane(g * (batch // LANES) + q, 1 - x), LANES)
            lanes = slice(q * LANES, (q + 1) * LANES)
            gram[:, place] = RG[g, :, lanes] * scale
            ham[:, place] = RH[g, :, lanes] * scale

    span = levels
    last_slot = SKEW * (chunks - 1) + span - 1
    work = {}

    def put(t, f, *args):
        work.setdefault(t, []).append(functools.partial(f, *args))

    put(span - 1, setup)
    for c in range(chunks):
        t = SKEW * c + span - 1
        put(t, stage_first, c)
        put(t, stage_filtered, c)
        for j in range(pieces):
            if ((j + 1) * LANES - 1) // chunk == c:
                put(t, panel_one, j)
                put(t + 1, panel_two, j)
                put(t + 2, panel_three, j)
    for c in range(chunks):
        put(SKEW * c + span, stage_image, c)
    for g in range(batches):
        need = ((g + 1) * batch - 1) // chunk
        t = SKEW * need + span + 1
        if g == 0:
            piece_slot = SKEW * ((pieces * LANES - 1) // chunk) + span + 2
            t = max(t, piece_slot)
            put(t, panel_ready)
            first_project = t
        put(max(t, first_project), project, g)

    for t in range(last_slot + 1):
        if t == 0:
            bundle_cross_wait()
        if 0 < t < levels:
            receives(bundle_hop, t - 1)
        if t < levels - 1:
            sends(bundle_hop, t, lambda copy: copy.start())
        for c in range(chunks):
            k = t - SKEW * c
            if 0 <= k < levels:
                if k == 0:
                    cross_wait(c)
                else:
                    receives(chunk_hop(c), k - 1)
                if k < levels - 1:
                    sends(chunk_hop(c), k, lambda copy: copy.start())
        for item in work.get(t, []):
            item()
    for t in sorted(work):
        if t > last_slot:
            for item in work[t]:
                item()
    for g in range(batches):
        collect(g)

    bundle_cross().wait_send()
    for c in range(chunks):
        cross(c).wait_send()
    for k in range(levels - 1):
        sends(bundle_hop, k, lambda copy: copy.wait_send())
        for c in range(chunks):
            sends(chunk_hop(c), k, lambda copy: copy.wait_send())
    panel_done()
    for g in range(batches):
        for copy in result_copies(g):
            copy.wait_send()


def shift_matrices(size, nz):
    row = jnp.arange(size)[:, None]
    col = jnp.arange(size)[None, :]
    same = row // nz == col // nz
    gap = (col - row) % nz
    near = jnp.where(same & ((gap == 1) | (gap == nz - 1)), -0.5, 0.0)
    lower = jnp.where(same & (gap == nz - TWIST), 1.0, 0.0)
    upper = jnp.where(same & (gap == TWIST), 1.0, 0.0)
    return jnp.stack([near, lower, upper]).astype(BF16)


def on_device(n, nb, orbitals, potential, near_points, near_values, far_points, far_values, atom_energy):
    _, nr, nz, cols = orbitals.shape
    plane = nr * nz
    atoms = near_points.shape[0]
    near = build_dense(near_points, near_values, plane).astype(F32)
    far = build_dense(far_points, far_values, plane).astype(F32)
    energy = jnp.broadcast_to(atom_energy[:, None], (atoms, plane))
    local = jnp.broadcast_to(potential.reshape(1, plane), (8, plane))
    bund = jnp.concatenate([near, far, energy, local], axis=0)
    shifts = shift_matrices(plane // 2, nz)
    mine = cols // 2
    chunk = LANES
    batch = min(2 * LANES, mine)
    chunks, batches = mine // chunk, mine // batch
    rows = PANEL // n
    panel_dev = PANEL // nb
    pieces = max(panel_dev // LANES // 2, 1)
    hops = n // 2 - 1
    tall = plane + 2 * nz
    vmem = pl.BlockSpec(memory_space=pltpu.VMEM)
    dma = pltpu.SemaphoreType.DMA
    return pl.pallas_call(
        functools.partial(kernel, n, nb, nr, nz, atoms, chunk, batch),
        out_shape=(jax.ShapeDtypeStruct((rows, cols), F32),) * 2,
        in_specs=[vmem] * 3,
        out_specs=(vmem,) * 2,
        scratch_shapes=[
            pltpu.VMEM((n + 2, tall, mine), BF16),
            pltpu.VMEM((n + 2, tall, chunk), BF16),
            pltpu.VMEM((n + 2, tall, mine), BF16),
            pltpu.VMEM((n, plane, mine), BF16),
            pltpu.VMEM((n,) + bund.shape, F32),
            pltpu.VMEM((n, 2 * atoms, plane), BF16),
            pltpu.VMEM((n, plane, LANES), BF16),
            pltpu.VMEM((n, plane, LANES), F32),
            pltpu.VMEM((n, 2 * atoms, chunk), F32),
            pltpu.VMEM((n, LANES, chunk), BF16),
            pltpu.VMEM((2, plane // 2, chunk), F32),
            pltpu.VMEM((n, plane, panel_dev), BF16),
            pltpu.VMEM((n, panel_dev, plane), BF16),
            pltpu.VMEM((batches, panel_dev, batch), F32),
            pltpu.VMEM((batches, panel_dev, batch), F32),
            pltpu.VMEM((batches, rows, batch), F32),
            pltpu.VMEM((batches, rows, batch), F32),
            dma((chunks,)),
            dma((chunks,)),
            dma((2, chunks, hops)),
            dma((2, chunks, hops)),
            dma,
            dma,
            dma((2, hops)),
            dma((2, hops)),
            dma((4, pieces, nb)),
            dma((4, pieces)),
            dma((2, batches)),
            dma((2, batches)),
        ],
        compiler_params=pltpu.CompilerParams(
            collective_id=0, has_side_effects=True, vmem_limit_bytes=60 * 2 ** 20
        ),
    )(orbitals.reshape(plane, cols), bund, shifts)


def solution(mesh):
    n, nb = mesh.shape["sector"], mesh.shape["band"]
    return jax.shard_map(
        functools.partial(on_device, n, nb),
        mesh=mesh,
        in_specs=(
            P("sector", None, None, "band"),
            P("sector", None, None),
            P("sector", None),
            P("sector", None),
            P("sector", None),
            P("sector", None),
            P("sector"),
        ),
        out_specs=(P("sector", "band"), P("sector", "band")),
        check_vma=False,
    )
```

```python
import functools

import jax
import jax.numpy as jnp
from jax import lax
from jax.experimental import pallas as pl
from jax.experimental.pallas import tpu as pltpu
from jax.sharding import PartitionSpec as P

MESH = pl.DeviceIdType.MESH
F32 = jnp.float32
BF16 = jnp.bfloat16

TWIST = 3
PANEL = 2048
CENTER = 6.0
HALF_SPAN = 3.0
LANES = 128
SKEW = 1


def build_dense(points, values, width):
    column_ids = jnp.arange(width, dtype=jnp.int32)
    matches = (points[:, :, None] == column_ids[None, None, :]).astype(F32)
    return jnp.sum(matches * values.astype(F32)[:, :, None], axis=1).astype(BF16)


def widen(tile, width):
    return jnp.concatenate([tile] * (width // LANES), axis=1) if width > LANES else tile


def kernel(n, nb, nr, nz, atoms, chunk, batch, orb, bund, shifts, ham, gram,
           O, A, F, I, BB, W, G, D, CO, SP, ACC, PB, PT, PH, PG, RH, RG,
           xs, xr, zs, zr, bxs, bxr, bzs, bzr, ps, pr, os, orr):
    plane, cols = orb.shape
    rows = ham.shape[0]
    half = plane // 2
    mine = cols // 2
    chunks = mine // chunk
    batches = mine // batch
    levels = n // 2
    panel_dev = PANEL // nb
    panel_blocks = panel_dev // LANES
    pieces = max(panel_blocks // 2, 1)
    both = panel_blocks >= 2
    order = list(range(pieces)) + ([panel_blocks + j for j in range(pieces)] if both else [])
    s = lax.axis_index("sector")
    b = lax.axis_index("band")
    x = lax.rem(s, 2)
    level = s // 2
    partner = s + 1 - 2 * x
    above, below = s + 2, s - 2
    core = lax.rem(b, 2)
    sibling = b + 1 - 2 * core
    owner = level

    def source_lane(j, side):
        return pl.multiple_of((order[j] + side * pieces) * LANES, LANES)

    def remote(src, dst, send, recv, **device):
        return pltpu.make_async_remote_copy(
            src_ref=src, dst_ref=dst, send_sem=send, recv_sem=recv, device_id=device, device_id_type=MESH)

    barrier = pltpu.get_barrier_semaphore()
    pl.semaphore_signal(barrier, inc=1, device_id={"sector": partner}, device_id_type=MESH)

    @pl.when(level < levels - 1)
    def _():
        pl.semaphore_signal(barrier, inc=1, device_id={"sector": above}, device_id_type=MESH)

    @pl.when(level > 0)
    def _():
        pl.semaphore_signal(barrier, inc=1, device_id={"sector": below}, device_id_type=MESH)

    for d in range(1, nb):
        pl.semaphore_signal(barrier, inc=1, device_id={"band": lax.rem(b + d, nb)}, device_id_type=MESH)

    for j in range(mine // LANES):
        O[s + 1, nz:nz + plane, j * LANES:(j + 1) * LANES] = orb[:, pl.ds(source_lane(j, x), LANES)]
    BB[s] = bund[...]
    ends = jnp.where(level == 0, 1, 0) + jnp.where(level == levels - 1, 1, 0)
    pl.semaphore_wait(barrier, nb + 2 - ends)

    per = chunk // LANES

    def cross(c):
        return remote(orb.at[:, pl.ds(source_lane(c * per, 1 - x), chunk)],
                      O.at[s + 1, pl.ds(nz, plane), pl.ds(c * chunk, chunk)],
                      xs.at[c], xr.at[c], sector=partner)

    def cross_wait(c):
        remote(orb.at[:, pl.ds(source_lane(c * per, x), chunk)],
               O.at[partner + 1, pl.ds(nz, plane), pl.ds(c * chunk, chunk)],
               xs.at[c], xr.at[c], sector=partner).wait_recv()

    def bundle_cross():
        return remote(BB.at[s], BB.at[s], bxs, bxr, sector=partner)

    def bundle_cross_wait():
        remote(BB.at[partner], BB.at[partner], bxs, bxr, sector=partner).wait_recv()

    def hop_parts(way, lv):
        if way == 0:
            return above
        return below

    def block_hop(c, lv, k, way):
        ref = O.at[pl.ds(2 * lv + 1, 2), pl.ds(nz, plane), pl.ds(c * chunk, chunk)]
        return remote(ref, ref, zs.at[way, c, k], zr.at[way, c, k], sector=hop_parts(way, lv))

    def bundle_hop(lv, k, way):
        ref = BB.at[pl.ds(2 * lv, 2)]
        return remote(ref, ref, bzs.at[way, k], bzr.at[way, k], sector=hop_parts(way, lv))

    def sends(make, k, act):
        @pl.when((level - k >= 0) & (level < levels - 1))
        def _():
            act(make(level - k, k, 0))

        @pl.when((level + k < levels) & (level > 0))
        def _():
            act(make(level + k, k, 1))

    def receives(make, k):
        @pl.when(level - 1 - k >= 0)
        def _():
            make(level - 1 - k, k, 0).wait_recv()

        @pl.when(level + 1 + k < levels)
        def _():
            make(level + 1 + k, k, 1).wait_recv()

    def chunk_hop(c):
        return functools.partial(block_hop, c)

    bundle_cross().start()
    for c in range(chunks):
        cross(c).start()

    for ref in (O, F):
        @pl.loop(0, n)
        def _(p):
            ref[p + 1, 0:nz, :] = jnp.zeros((nz, mine), BF16)
            ref[p + 1, nz + plane:nz + plane + nz, :] = jnp.zeros((nz, mine), BF16)

    @pl.loop(0, n)
    def _(p):
        A[p + 1, 0:nz, :] = jnp.zeros((nz, chunk), BF16)
        A[p + 1, nz + plane:nz + plane + nz, :] = jnp.zeros((nz, chunk), BF16)
        SP[p] = jnp.zeros(SP.shape[1:], BF16)

    def setup():
        @pl.loop(0, n)
        def _(p):
            dense = BB[p, 0:2 * atoms, :]
            W[p] = dense.astype(BF16)
            copies = LANES // (2 * atoms)
            G[p] = jnp.concatenate([dense] * copies, axis=0).T.astype(BF16)
            local = jnp.broadcast_to(BB[p, 3 * atoms:3 * atoms + 1, :], (LANES, plane)).T
            for i in range(nr):
                w = (nr / (nr + i)) ** 2
                D[p, i * nz:(i + 1) * nz, :] = local[i * nz:(i + 1) * nz] + (2.0 + w)

    def prepare(v, cs):
        for h in range(2):
            r = nz + h * half
            v[0, r:r + half, cs] = jnp.dot(shifts[1], v[n, r:r + half, cs], preferred_element_type=F32).astype(BF16)
            v[n + 1, r:r + half, cs] = jnp.dot(shifts[2], v[1, r:r + half, cs], preferred_element_type=F32).astype(BF16)

        @pl.loop(0, n, unroll=4)
        def _(p):
            CO[p] = jnp.dot(W[p], v[p + 1, nz:nz + plane, cs], preferred_element_type=F32)

        @pl.loop(0, n)
        def _(p):
            after = lax.rem(p + 1, n)
            energy = widen(BB[p, 2 * atoms:3 * atoms, 0:LANES], chunk)
            rest = energy * (CO[p, 0:atoms, :] + CO[after, atoms:2 * atoms, :])
            for term in range(3):
                part = rest.astype(BF16)
                rest = rest - part.astype(F32)
                r = term * 2 * atoms
                SP[p, r:r + atoms, :] = part
                SP[after, r + atoms:r + 2 * atoms, :] = part

    def operate(v, cs, finish):
        prepare(v, cs)

        @pl.loop(0, n)
        def _(p):
            for h in range(2):
                base = nz + h * half
                ACC[h] = (
                    jnp.dot(shifts[0], v[p + 1, base:base + half, cs], preferred_element_type=F32)
                    + jnp.dot(G[p, h * half:(h + 1) * half, :], SP[p], preferred_element_type=F32))
            inner = None
            centre = v[p + 1, nz:2 * nz, cs].astype(F32)
            for i in range(nr):
                ri = nr + i
                r = nz + i * nz
                q = i * nz - (half if i * nz >= half else 0)
                outer = v[p + 1, r + nz:r + 2 * nz, cs].astype(F32) if i < nr - 1 else None
                sides = v[p + 2, r:r + nz, cs].astype(F32) + v[p, r:r + nz, cs].astype(F32)
                local = widen(D[p, r - nz:r, :], chunk)
                value = (
                    ACC[i * nz // half, q:q + nz, :]
                    + (-0.5 * (nr / ri) ** 2) * sides
                    + local * centre)
                if outer is not None:
                    value = value + (-0.5 * (1.0 + 1.0 / (2.0 * ri))) * outer
                if inner is not None:
                    value = value + (-0.5 * (1.0 - 1.0 / (2.0 * ri))) * inner
                finish(p, r, centre, value)
                inner, centre = centre, outer

    def stage_first(c):
        cs = slice(c * chunk, (c + 1) * chunk)

        def finish(p, r, centre, value):
            A[p + 1, r:r + nz, :] = ((value - CENTER * centre) * (1.0 / HALF_SPAN)).astype(BF16)

        operate(O, cs, finish)

    def stage_filtered(c):
        cs = slice(c * chunk, (c + 1) * chunk)

        def finish(p, r, centre, value):
            start = O[p + 1, r:r + nz, cs].astype(F32)
            F[p + 1, r:r + nz, cs] = (
                (value - CENTER * centre) * (2.0 / HALF_SPAN) - start).astype(BF16)

        operate(A, slice(0, chunk), finish)

    def stage_image(c):
        cs = slice(c * chunk, (c + 1) * chunk)

        def finish(p, r, centre, value):
            I[p, r - nz:r, cs] = value.astype(BF16)

        operate(F, cs, finish)

    part = n // 2

    def panel_at(j, side, which):
        lane = pl.multiple_of((j + side * pieces) * LANES, LANES)
        return PB.at[pl.ds(which * part, part), :, pl.ds(lane, LANES)]

    def panel_out(j, d):
        to = lax.rem(b + d, nb)
        which = lax.rem(to, 2)
        return remote(F.at[pl.ds(1 + which * part, part), pl.ds(nz, plane), pl.ds(j * LANES, LANES)],
                      panel_at(j, x, which), ps.at[0, j, d], pr.at[0, j], band=to)

    def panel_cross(j, side):
        return remote(panel_at(j, side, core), panel_at(j, side, core), ps.at[1, j, 0], pr.at[1, j], sector=partner)

    def panel_pair(j, side, which, own):
        k = 2 if own else 3
        return remote(panel_at(j, side, which), panel_at(j, side, which), ps.at[k, j, 0], pr.at[k, j], band=sibling)

    def when_own(f):
        if both:
            f()
        else:
            pl.when(x == 0)(f)

    def when_other(f):
        if both:
            f()
        else:
            pl.when(x == 1)(f)

    def panel_one(j):
        def go():
            @pl.when(b == owner)
            def _():
                for d in range(1, nb):
                    panel_out(j, d).start()
                lane = pl.multiple_of((j + x * pieces) * LANES, LANES)

                @pl.loop(0, part)
                def _(p):
                    PB[core * part + p, :, pl.ds(lane, LANES)] = (
                        F[1 + core * part + p, nz:nz + plane, j * LANES:(j + 1) * LANES])
        when_own(go)

    def panel_two(j):
        def go():
            @pl.when(b != owner)
            def _():
                remote(panel_at(j, x, core), panel_at(j, x, core), ps.at[0, j, 0], pr.at[0, j], band=sibling).wait_recv()
            panel_cross(j, x).start()
            panel_pair(j, x, core, True).start()
        when_own(go)

    def panel_three(j):
        def go():
            panel_cross(j, 1 - x).wait_recv()
            panel_pair(j, 1 - x, core, False).start()
        when_other(go)

    def panel_ready():
        for j in range(pieces):
            when_own(lambda: panel_pair(j, x, 1 - core, True).wait_recv())
            when_other(lambda: panel_pair(j, 1 - x, 1 - core, False).wait_recv())

        @pl.loop(0, n)
        def _(p):
            PT[p] = PB[p].T

    def panel_done():
        for j in range(pieces):
            def own():
                @pl.when(b == owner)
                def _():
                    for d in range(1, nb):
                        panel_out(j, d).wait_send()
                panel_cross(j, x).wait_send()
                panel_pair(j, x, core, True).wait_send()
            when_own(own)
            when_other(lambda: panel_pair(j, 1 - x, core, False).wait_send())

    scale = 1.0 / (plane * n)

    def result_copies(g):
        theirs = pl.ds(pl.multiple_of((1 - x) * rows, 8), rows)
        return (remote(PH.at[g, theirs], RH.at[g], os.at[0, g], orr.at[0, g], sector=partner),
                remote(PG.at[g, theirs], RG.at[g], os.at[1, g], orr.at[1, g], sector=partner))

    def project(g):
        cs = slice(g * batch, (g + 1) * batch)
        PG[g] = jnp.dot(PT[0], F[1, nz:nz + plane, cs], preferred_element_type=F32)
        PH[g] = jnp.dot(PT[0], I[0, :, cs], preferred_element_type=F32)

        @pl.loop(1, n)
        def _(p):
            PG[g] += jnp.dot(PT[p], F[p + 1, nz:nz + plane, cs], preferred_element_type=F32)
            PH[g] += jnp.dot(PT[p], I[p, :, cs], preferred_element_type=F32)

        for copy in result_copies(g):
            copy.start()
        ours = pl.ds(pl.multiple_of(x * rows, 8), rows)
        for q in range(batch // LANES):
            place = pl.ds(source_lane(g * (batch // LANES) + q, x), LANES)
            lanes = slice(q * LANES, (q + 1) * LANES)
            gram[:, place] = PG[g, ours, lanes] * scale
            ham[:, place] = PH[g, ours, lanes] * scale

    def collect(g):
        for copy in result_copies(g):
            copy.wait_recv()
        for q in range(batch // LANES):
            place = pl.ds(source_lane(g * (batch // LANES) + q, 1 - x), LANES)
            lanes = slice(q * LANES, (q + 1) * LANES)
            gram[:, place] = RG[g, :, lanes] * scale
            ham[:, place] = RH[g, :, lanes] * scale

    span = levels
    last_slot = SKEW * (chunks - 1) + span - 1
    work = {}

    def put(t, f, *args):
        work.setdefault(t, []).append(functools.partial(f, *args))

    put(span - 1, setup)
    for c in range(chunks):
        t = SKEW * c + span - 1
        put(t, stage_first, c)
        put(t, stage_filtered, c)
        for j in range(pieces):
            if ((j + 1) * LANES - 1) // chunk == c:
                put(t, panel_one, j)
                put(t + 1, panel_two, j)
                put(t + 2, panel_three, j)
    for c in range(chunks):
        put(SKEW * c + span, stage_image, c)
    for g in range(batches):
        need = ((g + 1) * batch - 1) // chunk
        t = SKEW * need + span + 1
        if g == 0:
            piece_slot = SKEW * ((pieces * LANES - 1) // chunk) + span + 2
            t = max(t, piece_slot)
            put(t, panel_ready)
            first_project = t
        put(max(t, first_project), project, g)

    for t in range(last_slot + 1):
        if t == 0:
            bundle_cross_wait()
        if 0 < t < levels:
            receives(bundle_hop, t - 1)
        if t < levels - 1:
            sends(bundle_hop, t, lambda copy: copy.start())
        for c in range(chunks):
            k = t - SKEW * c
            if 0 <= k < levels:
                if k == 0:
                    cross_wait(c)
                else:
                    receives(chunk_hop(c), k - 1)
                if k < levels - 1:
                    sends(chunk_hop(c), k, lambda copy: copy.start())
        for item in work.get(t, []):
            item()
    for t in sorted(work):
        if t > last_slot:
            for item in work[t]:
                item()
    for g in range(batches):
        collect(g)

    bundle_cross().wait_send()
    for c in range(chunks):
        cross(c).wait_send()
    for k in range(levels - 1):
        sends(bundle_hop, k, lambda copy: copy.wait_send())
        for c in range(chunks):
            sends(chunk_hop(c), k, lambda copy: copy.wait_send())
    panel_done()
    for g in range(batches):
        for copy in result_copies(g):
            copy.wait_send()


def shift_matrices(size, nz):
    row = jnp.arange(size)[:, None]
    col = jnp.arange(size)[None, :]
    same = row // nz == col // nz
    gap = (col - row) % nz
    near = jnp.where(same & ((gap == 1) | (gap == nz - 1)), -0.5, 0.0)
    lower = jnp.where(same & (gap == nz - TWIST), 1.0, 0.0)
    upper = jnp.where(same & (gap == TWIST), 1.0, 0.0)
    return jnp.stack([near, lower, upper]).astype(BF16)


def on_device(n, nb, orbitals, potential, near_points, near_values, far_points, far_values, atom_energy):
    _, nr, nz, cols = orbitals.shape
    plane = nr * nz
    atoms = near_points.shape[0]
    near = build_dense(near_points, near_values, plane).astype(F32)
    far = build_dense(far_points, far_values, plane).astype(F32)
    energy = jnp.broadcast_to(atom_energy[:, None], (atoms, plane))
    local = jnp.broadcast_to(potential.reshape(1, plane), (8, plane))
    bund = jnp.concatenate([near, far, energy, local], axis=0)
    shifts = shift_matrices(plane // 2, nz)
    mine = cols // 2
    chunk = LANES
    batch = min(2 * LANES, mine)
    chunks, batches = mine // chunk, mine // batch
    rows = PANEL // n
    panel_dev = PANEL // nb
    pieces = max(panel_dev // LANES // 2, 1)
    hops = n // 2 - 1
    tall = plane + 2 * nz
    vmem = pl.BlockSpec(memory_space=pltpu.VMEM)
    dma = pltpu.SemaphoreType.DMA
    return pl.pallas_call(
        functools.partial(kernel, n, nb, nr, nz, atoms, chunk, batch),
        out_shape=(jax.ShapeDtypeStruct((rows, cols), F32),) * 2,
        in_specs=[vmem] * 3,
        out_specs=(vmem,) * 2,
        scratch_shapes=[
            pltpu.VMEM((n + 2, tall, mine), BF16),
            pltpu.VMEM((n + 2, tall, chunk), BF16),
            pltpu.VMEM((n + 2, tall, mine), BF16),
            pltpu.VMEM((n, plane, mine), BF16),
            pltpu.VMEM((n,) + bund.shape, F32),
            pltpu.VMEM((n, 2 * atoms, plane), BF16),
            pltpu.VMEM((n, plane, LANES), BF16),
            pltpu.VMEM((n, plane, LANES), F32),
            pltpu.VMEM((n, 2 * atoms, chunk), F32),
            pltpu.VMEM((n, LANES, chunk), BF16),
            pltpu.VMEM((2, plane // 2, chunk), F32),
            pltpu.VMEM((n, plane, panel_dev), BF16),
            pltpu.VMEM((n, panel_dev, plane), BF16),
            pltpu.VMEM((batches, panel_dev, batch), F32),
            pltpu.VMEM((batches, panel_dev, batch), F32),
            pltpu.VMEM((batches, rows, batch), F32),
            pltpu.VMEM((batches, rows, batch), F32),
            dma((chunks,)),
            dma((chunks,)),
            dma((2, chunks, hops)),
            dma((2, chunks, hops)),
            dma,
            dma,
            dma((2, hops)),
            dma((2, hops)),
            dma((4, pieces, nb)),
            dma((4, pieces)),
            dma((2, batches)),
            dma((2, batches)),
        ],
        compiler_params=pltpu.CompilerParams(
            collective_id=0, has_side_effects=True, vmem_limit_bytes=60 * 2 ** 20
        ),
    )(orbitals.reshape(plane, cols), bund, shifts)


def solution(mesh):
    n, nb = mesh.shape["sector"], mesh.shape["band"]
    return jax.shard_map(
        functools.partial(on_device, n, nb),
        mesh=mesh,
        in_specs=(
            P("sector", None, None, "band"),
            P("sector", None, None),
            P("sector", None),
            P("sector", None),
            P("sector", None),
            P("sector", None),
            P("sector"),
        ),
        out_specs=(P("sector", "band"), P("sector", "band")),
        check_vma=False,
    )
```
